512 devices in a mesh: row: 32 (over z, x_lo), col: 16 (over y, x_hi, core).
Axes of the slice: x: 4 (x_hi: 2, x_lo: 2; x = x_hi * 2 + x_lo), y: 4, z: 16, core: 2. Of those that a mesh axis runs over, the one named last changes fastest.
Arguments:
- x_window: bfloat16 [3, 2048, 512], P(None, 'row', 'col'), may hold values from -6 to 6
- y_window: float32 [3, 2048], P(None, 'row'), may hold values from -6 to 6
- block_order: int32 [3], replicated, may hold values from 0 to 2, each once
- diag_inverse: bfloat16 [3, 2048, 2048], P(None, 'row'), may hold values from -0.5 to 1.5, as said below
- panel_window: bfloat16 [3, 2048, 2048], P(None, 'row', 'col'), may hold values from -0.078125 to 0.078125
- panel_trail: bfloat16 [4096, 3, 2048], P('row', None, 'col'), may hold values from -0.078125 to 0.078125
- x_trail: bfloat16 [4096, 512], P('row', 'col'), may hold values from -6 to 6
- y_trail: float32 [4096], P('row'), may hold values from -6 to 6
Outputs:
- whitened: bfloat16 [3, 2048, 512], P(None, 'row', 'col')
- white_resp: bfloat16 [3, 2048], P(None, 'row')
- trail_rhs: float32 [4096, 512], P('row', 'col')
- trail_resp: float32 [4096], P('row')
- normal_part: float32 [512, 512], P('row')
- right_part: float32 [512], P('row')
The draws below stay inside these ranges and needn't reach their ends.
Inputs may be any that keep to these rules, and one draw needn't show every extreme that they name: Each diag_inverse[s] is lower triangular with a positive diagonal.
All inputs are finite; a program needn't handle non-finite values.
Results may differ from the reference program's by a relative error of at most 0.014.
Values may be sent and summed in bfloat16 or wider, within the bound.
A program may use at most 64 MiB of HBM per device.

```python
import math
import jax
import jax.numpy as jnp
from jax import lax

P_SIZE = 512
NB = 2048
S = 3
TRAIL = 4096
PAIRS = 3


def draw_diag_inverse(key, part):
    key_off, key_diag = jax.random.split(jax.random.fold_in(key, 11))
    rows = lax.broadcasted_iota(jnp.int32, (S, NB, NB), 1)
    columns = lax.broadcasted_iota(jnp.int32, (S, NB, NB), 2)
    below = jax.random.normal(key_off, (S, NB, NB), jnp.float32)
    below = jnp.clip(below * (0.6 / math.sqrt(NB)), -0.5, 0.5)
    middle = jax.random.uniform(key_diag, (S, NB, NB), jnp.float32, 0.625, 1.5)
    values = jnp.where(rows == columns, middle, jnp.where(columns < rows, below, 0.0))
    return values.astype(jnp.bfloat16)


def block_scale(stream_key, extent, pieces, smallest, top_value):
    factor_of = 1.0
    for position, parts in pieces:
        heights = jax.random.uniform(jax.random.fold_in(jax.random.fold_in(stream_key, 6), position), (parts,), jnp.float32, smallest / len(pieces), top_value / len(pieces))
        factor_of = factor_of * jnp.repeat(jnp.exp(heights), extent[position] // parts).reshape((-1,) + (1,) * (len(extent) - 1 - position))
    return factor_of


def bell_draw(key, extent, width, bound, cuts=(), kind=jnp.bfloat16):
    array = jax.random.normal(key, extent, jnp.float32) * width
    if len(cuts) > 0:
        array = block_scale(key, extent, cuts, -0.22, 0.18) * array
    return jnp.clip(array, min=-bound, max=bound).astype(kind)


def setup_inputs(seed: int = 0) -> dict:
    key_of = jax.random.split(jax.random.key(seed), 9)
    x_window = bell_draw(key_of[0], (S, NB, P_SIZE), 1.0, 6.0, ((1, 32), (2, 16)))
    y_window = bell_draw(key_of[1], (S, NB), 1.0, 6.0, ((1, 32),), jnp.float32)
    block_order = jax.random.permutation(key_of[2], S).astype(jnp.int32)
    diag_inverse = draw_diag_inverse(jax.random.fold_in(key_of[8], 71), 0)
    panel_window = bell_draw(key_of[4], (PAIRS, NB, NB), (S * NB) ** -0.5, 0.078125, ((1, 32), (2, 16)))
    panel_trail = bell_draw(key_of[5], (TRAIL, S, NB), (S * NB) ** -0.5, 0.078125, ((0, 32), (2, 16)))
    x_trail = bell_draw(key_of[6], (TRAIL, P_SIZE), 1.0, 6.0, ((0, 32), (1, 16)))
    y_trail = bell_draw(key_of[7], (TRAIL,), 1.0, 6.0, ((0, 32),), jnp.float32)
    return {"x_window": x_window, "y_window": y_window, "block_order": block_order, "diag_inverse": diag_inverse, "panel_window": panel_window, "panel_trail": panel_trail, "x_trail": x_trail, "y_trail": y_trail}


def reference(x_window, y_window, block_order, diag_inverse, panel_window, panel_trail, x_trail, y_trail):
    hp = lax.Precision.HIGHEST
    solved = []
    solved_resp = []
    for s in range(S):
        pending = lax.dynamic_index_in_dim(x_window, block_order[s], 0, keepdims=False).astype(jnp.float32)
        pending_resp = lax.dynamic_index_in_dim(y_window, block_order[s], 0, keepdims=False)
        for t in range(s):
            factor = panel_window[s * (s - 1) // 2 + t].astype(jnp.float32)
            pending = pending - jnp.dot(factor, solved[t].astype(jnp.float32), precision=hp)
            pending_resp = pending_resp - jnp.dot(factor, solved_resp[t].astype(jnp.float32), precision=hp)
        residual = pending.astype(jnp.bfloat16)
        resid_resp = pending_resp.astype(jnp.bfloat16)
        solved.append(jnp.dot(diag_inverse[s], residual, preferred_element_type=jnp.float32).astype(jnp.bfloat16))
        solved_resp.append(jnp.dot(diag_inverse[s], resid_resp, preferred_element_type=jnp.float32).astype(jnp.bfloat16))
    whitened = jnp.stack(solved)
    white_resp = jnp.stack(solved_resp)
    zall = whitened.astype(jnp.float32)
    wall = white_resp.astype(jnp.float32)

    def one_block(s, carry):
        total, total_resp = carry
        factor = lax.dynamic_index_in_dim(panel_trail, s, 1, keepdims=False).astype(jnp.float32)
        block = lax.dynamic_index_in_dim(zall, s, 0, keepdims=False)
        block_resp = lax.dynamic_index_in_dim(wall, s, 0, keepdims=False)
        total = total + jnp.dot(factor, block, precision=hp)
        total_resp = total_resp + jnp.dot(factor, block_resp, precision=hp)
        return total, total_resp

    start = (jnp.zeros((TRAIL, P_SIZE), jnp.float32), jnp.zeros((TRAIL,), jnp.float32))
    total, total_resp = lax.fori_loop(0, S, one_block, start)
    trail_rhs = x_trail.astype(jnp.float32) - total
    trail_resp = y_trail - total_resp
    flat = zall.reshape(S * NB, P_SIZE)
    flat_resp = wall.reshape(S * NB)
    normal_part = jnp.dot(flat.T, flat, precision=hp) / (S * NB)
    right_part = jnp.dot(flat.T, flat_resp, precision=hp) / (S * NB)
    return whitened, white_resp, trail_rhs, trail_resp, normal_part, right_part
```

```python
import jax
import jax.numpy as jnp
from jax import lax
from jax.experimental import pallas as pl
from jax.experimental.pallas import tpu as pltpu
from jax.sharding import PartitionSpec as P

MESH = pl.DeviceIdType.MESH
F32 = jnp.float32
BF16 = jnp.bfloat16


def dot_t(a, b):
    return lax.dot_general(a, b, (((1,), (1,)), ((), ())), preferred_element_type=F32)


def twice(a):
    return jnp.concatenate([a, a], axis=0)


def kernel(
    order,
    x_ref,
    y_ref,
    d_hbm,
    l_ref,
    t_ref,
    white_out,
    trail_out,
    normal_out,
    right_out,
    ubuf,
    fbuf,
    xt,
    dv,
    lv,
    tsrc,
    tv,
    ah,
    nb,
    ybuf,
    d_sem,
    us_sem,
    ur_sem,
    fs_sem,
    fr_sem,
    ls_sem,
    lr_sem,
    ts_sem,
    tr_sem,
    as_sem,
    ar_sem,
    ns_sem,
    nr_sem,
):
    row = lax.axis_index("row")
    col = lax.axis_index("col")
    z = row // 2
    xl = row % 2
    n_row, n_col = 32, 16

    def row_peer(k):
        half = k // 2
        return lax.rem(row + n_row // 2 + jnp.where(k % 2 == 0, half, n_row - half - 1), n_row)

    def col_peer(k):
        return lax.rem(col + 1 + k, n_col)

    load_d = pltpu.make_async_copy(d_hbm, dv, d_sem)
    load_d.start()
    barrier = pltpu.get_barrier_semaphore()

    def greet_row(k, carry):
        pl.semaphore_signal(barrier, inc=1, device_id={"row": row_peer(k)}, device_id_type=MESH)
        return carry

    def greet_col(k, carry):
        pl.semaphore_signal(barrier, inc=1, device_id={"col": col_peer(k)}, device_id_type=MESH)
        return carry

    lax.fori_loop(0, n_row - 1, greet_row, 0)
    lax.fori_loop(0, n_col - 1, greet_col, 0)

    lane = lax.broadcasted_iota(jnp.int32, (16, 128), 1)
    low = lane < 64
    mine = jnp.where(xl == 0, lane, 127 - lane) < 64
    lane1 = lax.broadcasted_iota(jnp.int32, (1, 128), 1)
    mine1 = jnp.where(xl == 0, lane1, 127 - lane1) < 64
    eye = (
        lax.broadcasted_iota(jnp.int32, (48, 32), 0) == lax.broadcasted_iota(jnp.int32, (48, 32), 1)
    ).astype(F32).astype(BF16)
    sub = lax.broadcasted_iota(jnp.int32, (48, 128), 0)

    ybuf[...] = jnp.zeros_like(ybuf)

    def stored(s):
        block = x_ref[order[s]]
        ybuf[s, 0:1, 0:64] = y_ref[order[s]]
        y = ybuf[s]
        y = y + pltpu.roll(y, 64, 1)
        return dot_t(eye, twice(block)) + jnp.where(sub >= 32, y[0:1, :], 0.0)

    def send(p, value):
        ubuf[p, row] = jnp.where(mine, value[0:16], value[16:32]).astype(BF16)
        fbuf[p, row] = jnp.where(mine1, value[32:33], 0.0)

        def push(k, carry):
            peer = {"row": row_peer(k)}
            pltpu.make_async_remote_copy(
                ubuf.at[p, row], ubuf.at[p, row], us_sem.at[p], ur_sem.at[p], peer, MESH
            ).start()
            pltpu.make_async_remote_copy(
                fbuf.at[p, row], fbuf.at[p, row], fs_sem.at[p], fr_sem.at[p], peer, MESH
            ).start()
            return carry

        lax.fori_loop(0, n_row - 1, push, 0)

    def await_bytes(ref, sem):
        pltpu.make_async_copy(ref, ref, sem).wait()

    def receive(p, slot):
        await_bytes(ubuf.at[p, 0 : n_row - 1], ur_sem.at[p])
        await_bytes(fbuf.at[p, 0 : n_row - 1], fr_sem.at[p])

        def unpack(k, carry):
            even = ubuf[p, 2 * k].astype(F32)
            odd = ubuf[p, 2 * k + 1].astype(F32)
            at = pl.ds(pl.multiple_of(128 * k, 128), 128)
            xt[slot, 0:16, at] = jnp.where(low, even, odd).astype(BF16)
            xt[slot, 16:32, at] = pltpu.roll(jnp.where(low, odd, even), 64, 1).astype(BF16)
            resp = fbuf[p, 2 * k] + fbuf[p, 2 * k + 1]
            xt[slot, 32:48, at] = jnp.broadcast_to(resp, (16, 128)).astype(BF16)
            return carry

        lax.fori_loop(0, n_row // 2, unpack, 0, unroll=4)

    def rounded(value):
        return value.astype(BF16).astype(F32)

    my_cols = pl.ds(pl.multiple_of(128 * col, 128), 128)

    def send_l():
        def push(k, carry):
            pltpu.make_async_remote_copy(
                l_ref, lv.at[:, :, my_cols], ls_sem, lr_sem, {"col": col_peer(k)}, MESH
            ).start()
            return carry

        lax.fori_loop(0, n_col - 1, push, 0)
        lv[:, :, my_cols] = l_ref[...]

    def send_t(s):
        def push(k, carry):
            pltpu.make_async_remote_copy(
                tsrc.at[s],
                tv.at[s, :, my_cols],
                ts_sem.at[s],
                tr_sem.at[s],
                {"col": col_peer(k)},
                MESH,
            ).start()
            return carry

        lax.fori_loop(0, n_col - 1, push, 0)
        tv[s, :, my_cols] = tsrc[s]

    half = pl.ds(pl.multiple_of(16 * xl, 16), 16)

    def send_a(s):
        @pl.when(col == z)
        def _():
            ah[s] = xt[s, half, :]

            def push(k, carry):
                pltpu.make_async_remote_copy(
                    ah.at[s], ah.at[s], as_sem.at[s], ar_sem.at[s], {"col": col_peer(k)}, MESH
                ).start()
                return carry

            lax.fori_loop(0, n_col - 1, push, 0)

    def receive_a(s):
        @pl.when(col != z)
        def _():
            await_bytes(ah.at[s], ar_sem.at[s])

    def trail_term(s):
        await_bytes(tv.at[s, :, 0 : 128 * (n_col - 1)], tr_sem.at[s])
        return dot_t(xt[s], tv[s])

    def gram_term(s):
        receive_a(s)
        left = ah[s]
        own = xt[s, 0:32, :]
        return dot_t(left, twice(twice(own))), dot_t(left, xt[s, 32:48, :])

    pending0 = stored(0)
    pending1 = stored(1)
    pending2 = stored(2)
    for s in range(3):
        tsrc[s] = t_ref[s]

    pl.semaphore_wait(barrier, n_row - 1 + n_col - 1)

    send(0, pending0)
    send_l()
    load_d.wait()
    receive(0, 3)
    white0 = rounded(dot_t(xt[3], twice(dv[0])))
    send(1, white0)
    white_out[0] = white0
    send_t(0)

    receive(1, 0)
    await_bytes(lv.at[:, :, 0 : 128 * (n_col - 1)], lr_sem)
    send(2, pending1 - dot_t(xt[0], twice(lv[0])))
    send_a(0)
    send_t(1)
    pending2 = pending2 - dot_t(xt[0], twice(lv[1]))

    receive(2, 3)
    white1 = rounded(dot_t(xt[3], twice(dv[1])))
    send(3, white1)
    white_out[1] = white1
    send_t(2)
    trail = trail_term(0)

    receive(3, 1)
    send(4, pending2 - dot_t(xt[1], twice(lv[2])))
    send_a(1)
    trail = trail + trail_term(1)
    gram, right = gram_term(0)

    receive(4, 3)
    white2 = rounded(dot_t(xt[3], twice(dv[2])))
    send(5, white2)
    white_out[2] = white2
    gram1, right1 = gram_term(1)

    receive(5, 2)
    send_a(2)
    trail_out[...] = trail + trail_term(2)
    gram2, right2 = gram_term(2)
    scale = 1.0 / 6144
    right_out[...] = (right + right1 + right2) * scale
    gram = (gram + gram1 + gram2) * scale
    nb[col] = jnp.where(lane // 32 == col % 4, gram, 0.0)

    def push_n(k, carry):
        pltpu.make_async_remote_copy(
            nb.at[col], nb.at[col], ns_sem, nr_sem, {"col": col_peer(k)}, MESH
        ).start()
        return carry

    lax.fori_loop(0, n_col - 1, push_n, 0)
    for p in range(6):
        await_bytes(ubuf.at[p, 0 : n_row - 1], us_sem.at[p])
        await_bytes(fbuf.at[p, 0 : n_row - 1], fs_sem.at[p])
    await_bytes(lv.at[:, :, 0 : 128 * (n_col - 1)], ls_sem)
    for s in range(3):
        await_bytes(tv.at[s, :, 0 : 128 * (n_col - 1)], ts_sem.at[s])

        @pl.when(col == z)
        def _():
            def drain(k, carry):
                await_bytes(ah.at[s], as_sem.at[s])
                return carry

            lax.fori_loop(0, n_col - 1, drain, 0)

    await_bytes(nb.at[0 : n_col - 1], ns_sem)
    await_bytes(nb.at[0 : n_col - 1], nr_sem)
    for j in range(4):
        normal_out[:, 128 * j : 128 * j + 128] = (
            nb[4 * j] + nb[4 * j + 1] + nb[4 * j + 2] + nb[4 * j + 3]
        )


def shards(
    x_window, y_window, block_order, diag_inverse, panel_window, panel_trail, x_trail, y_trail
):
    vmem = pl.BlockSpec(memory_space=pltpu.VMEM)
    dma = pltpu.SemaphoreType.DMA
    white, trail, normal, right = pl.pallas_call(
        kernel,
        name="substitution",
        out_shape=(
            jax.ShapeDtypeStruct((3, 48, 128), F32),
            jax.ShapeDtypeStruct((48, 128), F32),
            jax.ShapeDtypeStruct((16, 512), F32),
            jax.ShapeDtypeStruct((16, 16), F32),
        ),
        in_specs=[
            pl.BlockSpec(memory_space=pltpu.SMEM),
            vmem,
            vmem,
            pl.BlockSpec(memory_space=pl.ANY),
            vmem,
            vmem,
        ],
        out_specs=(vmem, vmem, vmem, vmem),
        scratch_shapes=[
            pltpu.VMEM((6, 32, 16, 128), BF16),
            pltpu.VMEM((6, 32, 1, 128), F32),
            pltpu.VMEM((4, 48, 2048), BF16),
            pltpu.VMEM((3, 64, 2048), BF16),
            pltpu.VMEM((3, 64, 2048), BF16),
            pltpu.VMEM((3, 128, 128), BF16),
            pltpu.VMEM((3, 128, 2048), BF16),
            pltpu.VMEM((3, 16, 2048), BF16),
            pltpu.VMEM((16, 16, 128), F32),
            pltpu.VMEM((3, 8, 128), F32),
            dma,
            dma((6,)),
            dma((6,)),
            dma((6,)),
            dma((6,)),
            dma,
            dma,
            dma((3,)),
            dma((3,)),
            dma((3,)),
            dma((3,)),
            dma,
            dma,
        ],
        compiler_params=pltpu.CompilerParams(
            collective_id=0, has_side_effects=True, vmem_limit_bytes=48 * 1024 * 1024
        ),
    )(
        block_order,
        x_window,
        y_window[:, None, :],
        diag_inverse,
        panel_window,
        panel_trail.transpose(1, 0, 2),
    )
    whitened = white[:, 0:32, 0:64].transpose(0, 2, 1).astype(BF16)
    white_resp = white[:, 32, 0:64].astype(BF16)
    trail_rhs = x_trail.astype(F32) - trail[0:32].T
    trail_resp = y_trail - trail[32]
    return whitened, white_resp, trail_rhs, trail_resp, normal, right[:, 0]


def solution(mesh):
    in_specs = (
        P(None, "row", "col"),
        P(None, "row"),
        P(),
        P(None, "row", None),
        P(None, "row", "col"),
        P("row", None, "col"),
        P("row", "col"),
        P("row"),
    )
    out_specs = (
        P(None, "row", "col"),
        P(None, "row"),
        P("row", "col"),
        P("row"),
        P("row", None),
        P("row"),
    )
    return jax.shard_map(shards, mesh=mesh, in_specs=in_specs, out_specs=out_specs, check_vma=False)
```

```python
import jax
import jax.numpy as jnp
from jax import lax
from jax.experimental import pallas as pl
from jax.experimental.pallas import tpu as pltpu
from jax.sharding import PartitionSpec as P

MESH = pl.DeviceIdType.MESH
F32 = jnp.float32
BF16 = jnp.bfloat16
NZ = 16
NC = 16
X1, W0, R2, W1, W2 = range(5)
WHITE = (W0, W1, W2)


def dot_t(a, b):
    return lax.dot_general(a, b, (((1,), (1,)), ((), ())), preferred_element_type=F32)


def dot_n(a, b):
    return lax.dot_general(a, b, (((1,), (0,)), ((), ())), preferred_element_type=F32)


def rounded(value):
    return value.astype(BF16).astype(F32)


def await_bytes(ref, sem):
    pltpu.make_async_copy(ref, ref, sem).wait()


def repeat(count, body):
    def step(k, carry):
        body(k)
        return carry

    lax.fori_loop(0, count, step, 0)


def kernel(
    order,
    x_ref,
    y_ref,
    d_ref,
    l_ref,
    t_ref,
    white_out,
    trail_out,
    normal_out,
    right_out,
    xsrc,
    ysrc,
    xbuf,
    ybuf,
    xr,
    ltsrc,
    ltex,
    lg,
    mv,
    gx,
    gy,
    hx,
    dv,
    lv,
    tv,
    ah,
    nb,
    tmp,
    own_sem,
    xs_sem,
    xr_sem,
    ys_sem,
    yr_sem,
    es_sem,
    er_sem,
    ds_sem,
    dr_sem,
    ls_sem,
    lr_sem,
    gs_sem,
    gr_sem,
    zs_sem,
    zr_sem,
    ms_sem,
    mr_sem,
    qs_sem,
    qr_sem,
    hs_sem,
    hr_sem,
    ts_sem,
    tr_sem,
    as_sem,
    ar_sem,
    ns_sem,
    nr_sem,
):
    row = lax.axis_index("row")
    c = lax.axis_index("col")
    z = row // 2
    x = row % 2
    spot = x * NC + c
    beside = {"row": 2 * z + 1 - x, "col": c}

    def far(k):
        half = (k + 1) // 2
        return lax.rem(z + NZ // 2 + jnp.where(k % 2 == 1, half, NZ - half), NZ)

    def along(k):
        return {"row": 2 * far(k) + x, "col": c}

    def across(k):
        return {"row": 2 * far(k) + 1 - x, "col": c}

    def turn(k):
        return {"row": row, "col": lax.rem(c + 1 + k, NC)}

    def over(k):
        return {"row": 2 * z + 1 - x, "col": lax.rem(c + k, NC)}

    def plane(k):
        other = lax.rem(spot + 1 + k, 2 * NC)
        return {"row": 2 * z + other // NC, "col": other % NC}

    def push(src, dst, send_sem, recv_sem, peer):
        pltpu.make_async_remote_copy(src, dst, send_sem, recv_sem, peer, MESH).start()

    at_c = pl.ds(pl.multiple_of(128 * c, 128), 128)
    at_z = pl.ds(pl.multiple_of(128 * z, 128), 128)
    own_half = pl.ds(pl.multiple_of(64 * x, 64), 64)
    other_half = pl.ds(pl.multiple_of(64 - 64 * x, 64), 64)

    barrier = pltpu.get_barrier_semaphore()

    def greet(peer):
        pl.semaphore_signal(barrier, inc=1, device_id=peer, device_id_type=MESH)

    repeat(NZ - 1, lambda k: greet(along(k)))
    repeat(NZ - 1, lambda k: greet(across(k)))
    repeat(2 * NC - 1, lambda k: greet(plane(k)))

    pltpu.make_async_copy(d_ref, dv.at[:, own_half, :], own_sem.at[0]).start()
    pltpu.make_async_copy(l_ref.at[1], lv.at[own_half, at_c], lr_sem).start()

    lane = lax.broadcasted_iota(jnp.int32, (16, 128), 1)
    first = x == 0
    mine = jnp.where(first, lane, 127 - lane) < 64
    mine1 = mine[0:1]

    tmp[...] = jnp.zeros_like(tmp)
    for s in range(3):
        tmp[0:32, 0:64] = x_ref[order[s]].astype(F32)
        tmp[32:33, 0:64] = y_ref[pl.ds(order[s], 1), :]
        both = tmp[...]
        both = jnp.where(first, both, pltpu.roll(both, 64, 1))
        xsrc[s, 0] = jnp.where(first, both[0:16], both[16:32]).astype(BF16)
        xsrc[s, 1] = jnp.where(first, both[16:32], both[0:16]).astype(BF16)
        ysrc[s] = both[32:33]
    eye = (
        lax.broadcasted_iota(jnp.int32, (128, 128), 0)
        == lax.broadcasted_iota(jnp.int32, (128, 128), 1)
    ).astype(F32).astype(BF16)
    lane_l = lax.broadcasted_iota(jnp.int32, (128, 128), 1)
    mine_l = jnp.where(first, lane_l, 127 - lane_l) < 64
    for q in range(2):
        block = l_ref[2 * q]
        turned = dot_t(eye, jnp.concatenate([block, block], axis=0))
        ltsrc[q] = jnp.where(mine_l, turned, 0.0).astype(BF16)

        def clear(k):
            @pl.when(k > z)
            def _():
                lg[q, :, pl.ds(pl.multiple_of(128 * k, 128), 128)] = jnp.zeros((64, 128), BF16)

        repeat(NZ, clear)

    xbuf[2, row] = xsrc[0, 0]
    ybuf[2, row] = ysrc[0]

    pl.semaphore_wait(barrier, 2 * (NZ - 1) + 2 * NC - 1)

    def push_x0(k):
        push(xsrc.at[0, 0], xbuf.at[2, row], xs_sem, xr_sem, along(k))
        push(xsrc.at[0, 1], xbuf.at[2, row], xs_sem, xr_sem, across(k))
        push(ysrc.at[0], ybuf.at[2, row], ys_sem, yr_sem, along(k))
        push(ysrc.at[0], ybuf.at[2, row], ys_sem, yr_sem, across(k))

    repeat(NZ - 1, push_x0)
    push(xsrc.at[0, 1], xbuf.at[2, row], xs_sem, xr_sem, beside)
    push(ysrc.at[0], ybuf.at[2, row], ys_sem, yr_sem, beside)
    for q in range(2):
        push(ltsrc.at[q, other_half], ltex.at[q], es_sem.at[q], er_sem.at[q], beside)
        if q == 0:
            push(xsrc.at[1:3, 1], xbuf.at[0:2, 0], es_sem.at[2], er_sem.at[2], beside)
            push(ysrc.at[1:3], ybuf.at[0:2, 0], es_sem.at[3], er_sem.at[3], beside)

    def push_d(s):
        def one(k):
            push(
                d_ref.at[s, :, at_c], dv.at[s, own_half, at_c], ds_sem.at[s], dr_sem.at[s], over(k)
            )

        repeat(NC, one)

    def push_lg(q):
        await_bytes(ltex.at[q], er_sem.at[q])
        lg[q, :, at_z] = ltsrc[q, own_half, :] + ltex[q]

        def one(k):
            @pl.when(far(k) > z)
            def _():
                push(
                    lg.at[q, :, at_z], lg.at[q, :, at_z], gs_sem.at[q], gr_sem.at[q, z], along(k)
                )

        repeat(NZ - 1, one)

    def form_m(q):
        def one(k):
            @pl.when(k < z)
            def _():
                await_bytes(
                    lg.at[q, :, pl.ds(pl.multiple_of(128 * k, 128), 128)], gr_sem.at[q, k]
                )

        repeat(NZ - 1, one)
        await_bytes(dv.at[1 + q, 0:64], dr_sem.at[1 + q])
        at = pl.ds(pl.multiple_of(128 * c + 64 * x, 64), 64)
        mv[q, at, :] = dot_t(lg[q], dv[1 + q]).astype(BF16)
        repeat(
            2 * NC - 1,
            lambda k: push(mv.at[q, at], mv.at[q, at], ms_sem.at[q], mr_sem.at[q], plane(k)),
        )

    def send(p, value):
        gx[p, 0:16, at_z] = value[0:16].astype(BF16)
        gy[p, :, at_z] = value[16:17]

        def one(k):
            push(gx.at[p, 0:16, at_z], gx.at[p, 0:16, at_z], zs_sem.at[p], zr_sem.at[p], along(k))
            push(gy.at[p, :, at_z], gy.at[p, :, at_z], qs_sem.at[p], qr_sem.at[p], along(k))
            if p == W2:
                push(gx.at[p, 0:16, at_z], hx.at[2, :, at_z], hs_sem.at[2], hr_sem.at[2], across(k))

        repeat(NZ - 1, one)
        if p == W2:
            push(gx.at[p, 0:16, at_z], hx.at[2, :, at_z], hs_sem.at[2], hr_sem.at[2], beside)

    def receive(p):
        await_bytes(gx.at[p, 0:16, 0 : 128 * (NZ - 1)], zr_sem.at[p])
        await_bytes(gy.at[p, :, 0 : 128 * (NZ - 1)], qr_sem.at[p])
        gx[p, 16:32, :] = jnp.broadcast_to(gy[p], (16, 128 * NZ)).astype(BF16)

    def push_t(s):
        def one(k):
            push(t_ref.at[s], tv.at[s, :, at_c], ts_sem.at[s], tr_sem.at[s], turn(k))

        repeat(NC - 1, one)
        tv[s, :, at_c] = t_ref[s]

    def push_h(s):
        push(gx.at[WHITE[s], 0:16], hx.at[s], hs_sem.at[s], hr_sem.at[s], beside)

    def push_a(s):
        @pl.when(c == z)
        def _():
            ah[s] = gx[WHITE[s], 0:16, :]
            repeat(
                NC - 1, lambda k: push(ah.at[s], ah.at[s], as_sem.at[s], ar_sem.at[s], turn(k))
            )

    def receive_h(s):
        await_bytes(hx.at[s], hr_sem.at[s])

    def put_white(s):
        own = gx[WHITE[s], 0:16, at_z].astype(F32)
        other = hx[s, :, at_z].astype(F32)
        resp = gx[WHITE[s], 16:32, at_z].astype(F32)
        value = jnp.concatenate(
            [jnp.where(first, own, other), jnp.where(first, other, own), resp], axis=0
        )
        white_out[s] = jnp.where(first, value, pltpu.roll(value, 64, 1))

    def trail_term(s):
        await_bytes(tv.at[s, :, 0 : 128 * (NC - 1)], tr_sem.at[s])
        return dot_t(jnp.concatenate([gx[WHITE[s]], hx[s]], axis=0), tv[s])

    def gram_term(s):
        @pl.when(c != z)
        def _():
            await_bytes(ah.at[s], ar_sem.at[s])

        left = ah[s]
        pair = jnp.concatenate([gx[WHITE[s], 0:16, :], hx[s]], axis=0)
        four = jnp.concatenate([pair, pair, pair, pair], axis=0)
        return dot_t(left, four), dot_t(left, gx[WHITE[s], 16:32, :])

    push_d(0)
    push_lg(0)
    push_d(1)
    await_bytes(xbuf.at[0:2, 0], er_sem.at[2])
    await_bytes(ybuf.at[0:2, 0], er_sem.at[3])
    tile1 = xsrc[1, 0].astype(F32) + xbuf[0, 0].astype(F32)
    resp1 = ysrc[1] + ybuf[0, 0]
    send(X1, jnp.concatenate([tile1, jnp.broadcast_to(resp1, (16, 128))], axis=0))
    tile2 = xsrc[2, 0].astype(F32) + xbuf[1, 0].astype(F32)
    resp2 = ysrc[2] + ybuf[1, 0]
    start2 = jnp.concatenate([tile2, jnp.broadcast_to(resp2, (16, 128))], axis=0)
    repeat(
        2 * NC - 1, lambda k: push(l_ref.at[1], lv.at[own_half, at_c], ls_sem, lr_sem, plane(k))
    )
    push_d(2)
    await_bytes(dv.at[:, 0:64, :], own_sem.at[0])

    await_bytes(xbuf.at[2, 0 : 2 * NZ - 1], xr_sem)
    await_bytes(ybuf.at[2, 0 : 2 * NZ - 1], yr_sem)
    for k in range(NZ):
        xr[0:16, 128 * k : 128 * k + 128] = xbuf[2, 2 * k] + xbuf[2, 2 * k + 1]
        xr[16:32, 128 * k : 128 * k + 128] = jnp.broadcast_to(
            ybuf[2, 2 * k] + ybuf[2, 2 * k + 1], (16, 128)
        ).astype(BF16)
    await_bytes(dv.at[0, 0:64], dr_sem.at[0])
    send(W0, rounded(dot_t(xr[...], dv[0])))
    push_lg(1)
    form_m(0)
    push_t(0)
    receive(X1)
    value1 = dot_t(gx[X1], dv[1])

    receive(W0)
    await_bytes(mv.at[0, 0 : 64 * (2 * NC - 1)], mr_sem.at[0])
    send(W1, rounded(value1 - dot_n(gx[W0], mv[0])))
    await_bytes(lv, lr_sem)
    send(R2, start2 - dot_t(gx[W0], lv[...]))
    push_h(0)
    push_a(0)
    form_m(1)
    push_t(1)
    push_t(2)
    receive_h(0)
    put_white(0)
    trail = trail_term(0)

    receive(R2)
    value2 = dot_t(gx[R2], dv[2])
    receive(W1)
    await_bytes(mv.at[1, 0 : 64 * (2 * NC - 1)], mr_sem.at[1])
    send(W2, rounded(value2 - dot_n(gx[W1], mv[1])))
    push_h(1)
    push_a(1)
    gram, right = gram_term(0)
    receive_h(1)
    put_white(1)
    trail = trail + trail_term(1)
    gram1, right1 = gram_term(1)

    receive(W2)
    push_a(2)
    receive_h(2)
    put_white(2)
    trail = trail + trail_term(2)
    trail_out[0:16] = jnp.where(first, trail[0:16], trail[32:48])
    trail_out[16:32] = jnp.where(first, trail[32:48], trail[0:16])
    trail_out[32:48] = trail[16:32]
    gram2, right2 = gram_term(2)
    scale = 1.0 / 6144
    right_out[...] = (right + right1 + right2) * scale
    gram = (gram + gram1 + gram2) * scale
    gram = jnp.where(first, gram, pltpu.roll(gram, 16, 1))
    nb[c] = jnp.where(lane // 32 == c % 4, gram, 0.0)
    repeat(NC - 1, lambda k: push(nb.at[c], nb.at[c], ns_sem, nr_sem, turn(k)))

    await_bytes(xbuf.at[2, 0 : 2 * NZ - 1], xs_sem)
    await_bytes(ybuf.at[2, 0 : 2 * NZ - 1], ys_sem)
    for q in range(2):
        await_bytes(ltex.at[q], es_sem.at[q])
        repeat(NZ - 1 - z, lambda k: await_bytes(lg.at[q, :, 0:128], gs_sem.at[q]))
        await_bytes(mv.at[q, 0 : 64 * (2 * NC - 1)], ms_sem.at[q])
    await_bytes(xbuf.at[0:2, 0], es_sem.at[2])
    await_bytes(ybuf.at[0:2, 0], es_sem.at[3])
    repeat(2 * NC - 1, lambda k: await_bytes(lv.at[0:64, 0:128], ls_sem))
    for p in range(5):
        await_bytes(gx.at[p, 0:16, 0 : 128 * (NZ - 1)], zs_sem.at[p])
        await_bytes(gy.at[p, :, 0 : 128 * (NZ - 1)], qs_sem.at[p])
    for s in range(3):
        await_bytes(dv.at[s, 0:64], ds_sem.at[s])
        await_bytes(hx.at[s], hs_sem.at[s])
        await_bytes(tv.at[s, :, 0 : 128 * (NC - 1)], ts_sem.at[s])

        @pl.when(c == z)
        def _():
            repeat(NC - 1, lambda k: await_bytes(ah.at[s], as_sem.at[s]))

    await_bytes(nb.at[0 : NC - 1], ns_sem)
    await_bytes(nb.at[0 : NC - 1], nr_sem)
    for j in range(4):
        normal_out[:, 128 * j : 128 * j + 128] = (
            nb[4 * j] + nb[4 * j + 1] + nb[4 * j + 2] + nb[4 * j + 3]
        )


def shards(
    x_window, y_window, block_order, diag_inverse, panel_window, panel_trail, x_trail, y_trail
):
    vmem = pl.BlockSpec(memory_space=pltpu.VMEM)
    hbm = pl.BlockSpec(memory_space=pl.ANY)
    dma = pltpu.SemaphoreType.DMA
    white, trail, normal, right = pl.pallas_call(
        kernel,
        name="substitution",
        out_shape=(
            jax.ShapeDtypeStruct((3, 48, 128), F32),
            jax.ShapeDtypeStruct((48, 128), F32),
            jax.ShapeDtypeStruct((16, 512), F32),
            jax.ShapeDtypeStruct((16, 16), F32),
        ),
        in_specs=[pl.BlockSpec(memory_space=pltpu.SMEM), vmem, vmem, hbm, vmem, vmem],
        out_specs=(vmem, vmem, vmem, vmem),
        scratch_shapes=[
            pltpu.VMEM((3, 2, 16, 128), BF16),
            pltpu.VMEM((3, 1, 128), F32),
            pltpu.VMEM((3, 32, 16, 128), BF16),
            pltpu.VMEM((3, 32, 1, 128), F32),
            pltpu.VMEM((32, 2048), BF16),
            pltpu.VMEM((2, 128, 128), BF16),
            pltpu.VMEM((2, 64, 128), BF16),
            pltpu.VMEM((2, 64, 2048), BF16),
            pltpu.VMEM((2, 2048, 128), BF16),
            pltpu.VMEM((5, 32, 2048), BF16),
            pltpu.VMEM((5, 1, 2048), F32),
            pltpu.VMEM((3, 16, 2048), BF16),
            pltpu.VMEM((3, 128, 2048), BF16),
            pltpu.VMEM((128, 2048), BF16),
            pltpu.VMEM((3, 128, 2048), BF16),
            pltpu.VMEM((3, 16, 2048), BF16),
            pltpu.VMEM((16, 16, 128), F32),
            pltpu.VMEM((40, 128), F32),
            dma((1,)),
            dma,
            dma,
            dma,
            dma,
            dma((4,)),
            dma((4,)),
            dma((3,)),
            dma((3,)),
            dma,
            dma,
            dma((2,)),
            dma((2, 16)),
            dma((5,)),
            dma((5,)),
            dma((2,)),
            dma((2,)),
            dma((5,)),
            dma((5,)),
            dma((3,)),
            dma((3,)),
            dma((3,)),
            dma((3,)),
            dma((3,)),
            dma((3,)),
            dma,
            dma,
        ],
        compiler_params=pltpu.CompilerParams(
            collective_id=0, has_side_effects=True, vmem_limit_bytes=58 * 1024 * 1024
        ),
    )(
        block_order,
        x_window.transpose(0, 2, 1),
        y_window,
        diag_inverse,
        panel_window,
        panel_trail.transpose(1, 0, 2),
    )
    whitened = white[:, 0:32, 0:64].transpose(0, 2, 1).astype(BF16)
    white_resp = white[:, 32, 0:64].astype(BF16)
    trail_rhs = x_trail.astype(F32) - trail[0:32].T
    trail_resp = y_trail - trail[32]
    return whitened, white_resp, trail_rhs, trail_resp, normal, right[:, 0]


def solution(mesh):
    in_specs = (
        P(None, "row", "col"),
        P(None, "row"),
        P(),
        P(None, "row", None),
        P(None, "row", "col"),
        P("row", None, "col"),
        P("row", "col"),
        P("row"),
    )
    out_specs = (
        P(None, "row", "col"),
        P(None, "row"),
        P("row", "col"),
        P("row"),
        P("row", None),
        P("row"),
    )
    return jax.shard_map(shards, mesh=mesh, in_specs=in_specs, out_specs=out_specs, check_vma=False)
```

```python
import jax
import jax.numpy as jnp
from jax import lax
from jax.experimental import pallas as pl
from jax.experimental.pallas import tpu as pltpu
from jax.sharding import PartitionSpec as P

MESH = pl.DeviceIdType.MESH
F32 = jnp.float32
BF16 = jnp.bfloat16
NZ = 16
NC = 16
W0, R1, R2, W1, W2 = range(5)
WHITE = (W0, W1, W2)


def dot_t(a, b):
    return lax.dot_general(a, b, (((1,), (1,)), ((), ())), preferred_element_type=F32)


def dot_n(a, b):
    return lax.dot_general(a, b, (((1,), (0,)), ((), ())), preferred_element_type=F32)


def rounded(value):
    return value.astype(BF16).astype(F32)


def await_bytes(ref, sem):
    pltpu.make_async_copy(ref, ref, sem).wait()


def repeat(count, body):
    def step(k, carry):
        body(k)
        return carry

    lax.fori_loop(0, count, step, 0)


def kernel(
    order,
    x_ref,
    y_ref,
    d_ref,
    l_ref,
    t_ref,
    white_out,
    trail_out,
    normal_out,
    right_out,
    xsrc,
    ysrc,
    xbuf,
    ybuf,
    xr,
    ltsrc,
    ltex,
    lg,
    mv,
    gx,
    gy,
    hx,
    dv,
    lv,
    tv,
    wp,
    gp,
    gq,
    nb,
    tmp,
    own_sem,
    xs_sem,
    xr_sem,
    ys_sem,
    yr_sem,
    es_sem,
    er_sem,
    ds_sem,
    dr_sem,
    ls_sem,
    lr_sem,
    gs_sem,
    gr_sem,
    zs_sem,
    zr_sem,
    ms_sem,
    mr_sem,
    qs_sem,
    qr_sem,
    hs_sem,
    hr_sem,
    ts_sem,
    tr_sem,
    vs_sem,
    vr_sem,
    as_sem,
    ar_sem,
    rs_sem,
    rr_sem,
    ns_sem,
    nr_sem,
):
    row = lax.axis_index("row")
    c = lax.axis_index("col")
    z = row // 2
    x = row % 2
    spot = x * NC + c
    beside = {"row": 2 * z + 1 - x, "col": c}

    def far(k):
        half = (k + 1) // 2
        return lax.rem(z + NZ // 2 + jnp.where(k % 2 == 1, half, NZ - half), NZ)

    def along(k):
        return {"row": 2 * far(k) + x, "col": c}

    def across(k):
        return {"row": 2 * far(k) + 1 - x, "col": c}

    def turn(k):
        return {"row": row, "col": lax.rem(c + 1 + k, NC)}

    def alike(k):
        return lax.rem(c + 2 + 2 * k, NC)

    sibling = {"row": row, "col": c + 1 - 2 * (c % 2)}

    def over(k):
        return {"row": 2 * z + 1 - x, "col": lax.rem(c + k, NC)}

    def plane(k):
        other = lax.rem(spot + 1 + k, 2 * NC)
        return {"row": 2 * z + other // NC, "col": other % NC}

    def push(src, dst, send_sem, recv_sem, peer):
        pltpu.make_async_remote_copy(src, dst, send_sem, recv_sem, peer, MESH).start()

    at_c = pl.ds(pl.multiple_of(128 * c, 128), 128)
    at_z = pl.ds(pl.multiple_of(128 * z, 128), 128)
    own_half = pl.ds(pl.multiple_of(64 * x, 64), 64)
    other_half = pl.ds(pl.multiple_of(64 - 64 * x, 64), 64)

    barrier = pltpu.get_barrier_semaphore()

    def greet(peer):
        pl.semaphore_signal(barrier, inc=1, device_id=peer, device_id_type=MESH)

    repeat(NZ - 1, lambda k: greet(along(k)))
    repeat(NZ - 1, lambda k: greet(across(k)))
    repeat(2 * NC - 1, lambda k: greet(plane(k)))

    pltpu.make_async_copy(d_ref, dv.at[:, own_half, :], own_sem.at[0]).start()
    for t in range(2):
        pltpu.make_async_copy(l_ref.at[t], lv.at[t, own_half, at_c], lr_sem.at[t]).start()

    lane = lax.broadcasted_iota(jnp.int32, (16, 128), 1)
    first = x == 0
    mine = jnp.where(first, lane, 127 - lane) < 64
    mine1 = mine[0:1]

    tmp[...] = jnp.zeros_like(tmp)
    for s in range(3):
        tmp[0:32, 0:64] = x_ref[order[s]].astype(F32)
        tmp[32:33, 0:64] = y_ref[pl.ds(order[s], 1), :]
        both = tmp[...]
        both = jnp.where(first, both, pltpu.roll(both, 64, 1))
        xsrc[s, 0] = jnp.where(first, both[0:16], both[16:32]).astype(BF16)
        xsrc[s, 1] = jnp.where(first, both[16:32], both[0:16]).astype(BF16)
        ysrc[s] = both[32:33]
    eye = (
        lax.broadcasted_iota(jnp.int32, (128, 128), 0)
        == lax.broadcasted_iota(jnp.int32, (128, 128), 1)
    ).astype(F32).astype(BF16)
    lane_l = lax.broadcasted_iota(jnp.int32, (128, 128), 1)
    mine_l = jnp.where(first, lane_l, 127 - lane_l) < 64
    block = l_ref[2]
    turned = dot_t(eye, jnp.concatenate([block, block], axis=0))
    ltsrc[...] = jnp.where(mine_l, turned, 0.0).astype(BF16)

    def clear(k):
        @pl.when(k > z)
        def _():
            lg[:, pl.ds(pl.multiple_of(128 * k, 128), 128)] = jnp.zeros((64, 128), BF16)

    repeat(NZ, clear)

    xbuf[2, row] = xsrc[0, 0]
    ybuf[2, row] = ysrc[0]

    pl.semaphore_wait(barrier, 2 * (NZ - 1) + 2 * NC - 1)

    def push_x0(k):
        push(xsrc.at[0, 0], xbuf.at[2, row], xs_sem, xr_sem, along(k))
        push(xsrc.at[0, 1], xbuf.at[2, row], xs_sem, xr_sem, across(k))
        push(ysrc.at[0], ybuf.at[2, row], ys_sem, yr_sem, along(k))
        push(ysrc.at[0], ybuf.at[2, row], ys_sem, yr_sem, across(k))

    repeat(NZ - 1, push_x0)
    push(xsrc.at[0, 1], xbuf.at[2, row], xs_sem, xr_sem, beside)
    push(ysrc.at[0], ybuf.at[2, row], ys_sem, yr_sem, beside)
    push(ltsrc.at[other_half], ltex, es_sem.at[0], er_sem.at[0], beside)
    push(xsrc.at[1:3, 1], xbuf.at[0:2, 0], es_sem.at[2], er_sem.at[2], beside)
    push(ysrc.at[1:3], ybuf.at[0:2, 0], es_sem.at[3], er_sem.at[3], beside)

    def push_d(s):
        def one(k):
            push(
                d_ref.at[s, :, at_c], dv.at[s, own_half, at_c], ds_sem.at[s], dr_sem.at[s], over(k)
            )

        repeat(NC, one)

    def push_lg():
        await_bytes(ltex, er_sem.at[0])
        lg[:, at_z] = ltsrc[own_half, :] + ltex[...]

        def one(k):
            @pl.when(far(k) > z)
            def _():
                push(lg.at[:, at_z], lg.at[:, at_z], gs_sem, gr_sem.at[z], along(k))

        repeat(NZ - 1, one)

    def push_l(t):
        repeat(
            2 * NC - 1,
            lambda k: push(
                l_ref.at[t], lv.at[t, own_half, at_c], ls_sem.at[t], lr_sem.at[t], plane(k)
            ),
        )

    def form_m():
        def one(k):
            @pl.when(k < z)
            def _():
                await_bytes(lg.at[:, pl.ds(pl.multiple_of(128 * k, 128), 128)], gr_sem.at[k])

        repeat(NZ - 1, one)
        await_bytes(dv.at[2, 0:64], dr_sem.at[2])
        at = pl.ds(pl.multiple_of(128 * c + 64 * x, 64), 64)
        mv[at, :] = dot_t(lg[...], dv[2]).astype(BF16)
        repeat(2 * NC - 1, lambda k: push(mv.at[at], mv.at[at], ms_sem, mr_sem, plane(k)))

    def push_a(s):
        p = WHITE[s]
        pltpu.make_async_copy(gx.at[p, 0:16, at_z], wp.at[s, c, x], ar_sem.at[s]).start()
        repeat(
            2 * NC - 1,
            lambda k: push(
                gx.at[p, 0:16, at_z], wp.at[s, c, x], as_sem.at[s], ar_sem.at[s], plane(k)
            ),
        )

    def send(p, value):
        gx[p, 0:16, at_z] = value[0:16].astype(BF16)
        gy[p, :, at_z] = value[16:17]

        if p == W2:
            push_a(2)

        def one(k):
            push(gx.at[p, 0:16, at_z], gx.at[p, 0:16, at_z], zs_sem.at[p], zr_sem.at[p], along(k))
            push(gy.at[p, :, at_z], gy.at[p, :, at_z], qs_sem.at[p], qr_sem.at[p], along(k))
            if p == W2:
                push(gx.at[p, 0:16, at_z], hx.at[2, :, at_z], hs_sem.at[2], hr_sem.at[2], across(k))

        repeat(NZ - 1, one)
        if p == W2:
            push(gx.at[p, 0:16, at_z], hx.at[2, :, at_z], hs_sem.at[2], hr_sem.at[2], beside)

    def receive(p):
        await_bytes(gx.at[p, 0:16, 0 : 128 * (NZ - 1)], zr_sem.at[p])
        await_bytes(gy.at[p, :, 0 : 128 * (NZ - 1)], qr_sem.at[p])
        gx[p, 16:32, :] = jnp.broadcast_to(gy[p], (16, 128 * NZ)).astype(BF16)

    def push_t(s):
        def one(k):
            peer = {"row": row, "col": alike(k)}
            push(t_ref.at[s], tv.at[s, :, at_c], ts_sem.at[s], tr_sem.at[s], peer)

        repeat(NC // 2 - 1, one)
        push(t_ref.at[s], tv.at[s, :, at_c], vs_sem.at[s], vr_sem.at[s], sibling)
        tv[s, :, at_c] = t_ref[s]

    def relay_t(s):
        await_bytes(tv.at[s, :, 0 : 128 * (NC // 2 - 1)], tr_sem.at[s])

        def one(k):
            at = pl.ds(pl.multiple_of(128 * alike(k), 128), 128)
            push(tv.at[s, :, at], tv.at[s, :, at], vs_sem.at[s], vr_sem.at[s], sibling)

        repeat(NC // 2 - 1, one)

    def push_h(s):
        push(gx.at[WHITE[s], 0:16], hx.at[s], hs_sem.at[s], hr_sem.at[s], beside)

    def receive_h(s):
        await_bytes(hx.at[s], hr_sem.at[s])

    def put_white(s):
        own = gx[WHITE[s], 0:16, at_z].astype(F32)
        other = hx[s, :, at_z].astype(F32)
        resp = gx[WHITE[s], 16:32, at_z].astype(F32)
        value = jnp.concatenate(
            [jnp.where(first, own, other), jnp.where(first, other, own), resp], axis=0
        )
        white_out[s] = jnp.where(first, value, pltpu.roll(value, 64, 1))

    def trail_term(s):
        await_bytes(tv.at[s, :, 0 : 128 * (NC // 2)], vr_sem.at[s])
        return dot_t(jnp.concatenate([gx[WHITE[s]], hx[s]], axis=0), tv[s])

    def gram_term(s):
        await_bytes(wp.at[s], ar_sem.at[s])
        left = wp[s, :, x].reshape(256, 128)
        own = wp[s, c].reshape(32, 128).astype(F32)
        resp = jnp.broadcast_to(gy[WHITE[s], :, at_z], (32, 128))
        groups = [jnp.where(c % 4 == j, own, resp) for j in range(4)]
        return dot_t(left, jnp.concatenate(groups, axis=0).astype(BF16))

    push_d(0)
    push_l(0)
    push_lg()
    await_bytes(xbuf.at[0:2, 0], er_sem.at[2])
    await_bytes(ybuf.at[0:2, 0], er_sem.at[3])
    starts = []
    for s in range(1, 3):
        tile = xsrc[s, 0].astype(F32) + xbuf[s - 1, 0].astype(F32)
        resp = jnp.broadcast_to(ysrc[s] + ybuf[s - 1, 0], (16, 128))
        starts.append(jnp.concatenate([tile, resp], axis=0))
    await_bytes(dv.at[:, 0:64, :], own_sem.at[0])

    await_bytes(xbuf.at[2, 0 : 2 * NZ - 1], xr_sem)
    await_bytes(ybuf.at[2, 0 : 2 * NZ - 1], yr_sem)
    for k in range(NZ):
        xr[0:16, 128 * k : 128 * k + 128] = xbuf[2, 2 * k] + xbuf[2, 2 * k + 1]
        xr[16:32, 128 * k : 128 * k + 128] = jnp.broadcast_to(
            ybuf[2, 2 * k] + ybuf[2, 2 * k + 1], (16, 128)
        ).astype(BF16)
    await_bytes(dv.at[0, 0:64], dr_sem.at[0])
    send(W0, rounded(dot_t(xr[...], dv[0])))
    push_d(1)
    push_l(1)
    push_d(2)
    push_a(0)

    receive(W0)
    await_bytes(lv.at[0], lr_sem.at[0])
    send(R1, starts[0] - dot_t(gx[W0], lv[0]))
    form_m()
    await_bytes(lv.at[1], lr_sem.at[1])
    send(R2, starts[1] - dot_t(gx[W0], lv[1]))
    push_h(0)

    await_bytes(dv.at[1, 0:64], dr_sem.at[1])
    receive(R1)
    send(W1, rounded(dot_t(gx[R1], dv[1])))
    push_a(1)
    for s in range(3):
        push_t(s)
    receive(R2)
    value2 = dot_t(gx[R2], dv[2])
    receive_h(0)
    put_white(0)
    gram = gram_term(0)

    receive(W1)
    await_bytes(mv.at[0 : 64 * (2 * NC - 1)], mr_sem)
    send(W2, rounded(value2 - dot_n(gx[W1], mv[...])))
    push_h(1)
    gram = gram + gram_term(1)

    gram = (gram + gram_term(2)) * (1.0 / 6144)
    gp[...] = gram.reshape(16, 16, 128)
    repeat(NZ - 1, lambda k: push(gp.at[far(k)], gq.at[z], rs_sem, rr_sem, along(k)))
    gq[z] = gp[z]
    for s in range(3):
        relay_t(s)
    trail = trail_term(0)
    receive_h(1)
    put_white(1)
    trail = trail + trail_term(1)

    receive(W2)
    receive_h(2)
    put_white(2)
    trail = trail + trail_term(2)
    trail_out[0:16] = jnp.where(first, trail[0:16], trail[32:48])
    trail_out[16:32] = jnp.where(first, trail[32:48], trail[0:16])
    trail_out[32:48] = trail[16:32]
    await_bytes(gq.at[0 : NZ - 1], rr_sem)
    gram = gq[0]
    for k in range(1, NZ):
        gram = gram + gq[k]
    nb[c] = jnp.where(lane // 32 == c % 4, gram, 0.0)
    repeat(NC - 1, lambda k: push(nb.at[c], nb.at[c], ns_sem, nr_sem, turn(k)))
    spare = jnp.where(c % 4 == 0, 32, 0)
    right = jnp.sum(jnp.where(lane == spare, gram, 0.0), axis=1, keepdims=True)
    right_out[...] = jnp.broadcast_to(right, (16, 128))
    await_bytes(gq.at[0 : NZ - 1], rs_sem)

    await_bytes(xbuf.at[2, 0 : 2 * NZ - 1], xs_sem)
    await_bytes(ybuf.at[2, 0 : 2 * NZ - 1], ys_sem)
    await_bytes(ltex, es_sem.at[0])
    repeat(NZ - 1 - z, lambda k: await_bytes(lg.at[:, 0:128], gs_sem))
    await_bytes(mv.at[0 : 64 * (2 * NC - 1)], ms_sem)
    await_bytes(xbuf.at[0:2, 0], es_sem.at[2])
    await_bytes(ybuf.at[0:2, 0], es_sem.at[3])
    for t in range(2):
        repeat(2 * NC - 1, lambda k: await_bytes(lv.at[t, 0:64, 0:128], ls_sem.at[t]))
    for p in range(5):
        await_bytes(gx.at[p, 0:16, 0 : 128 * (NZ - 1)], zs_sem.at[p])
        await_bytes(gy.at[p, :, 0 : 128 * (NZ - 1)], qs_sem.at[p])
    for s in range(3):
        await_bytes(dv.at[s, 0:64], ds_sem.at[s])
        await_bytes(hx.at[s], hs_sem.at[s])
        await_bytes(tv.at[s, :, 0 : 128 * (NC // 2 - 1)], ts_sem.at[s])
        await_bytes(tv.at[s, :, 0 : 128 * (NC // 2)], vs_sem.at[s])

        repeat(2 * NC - 1, lambda k: await_bytes(wp.at[s, 0, 0], as_sem.at[s]))

    await_bytes(nb.at[0 : NC - 1], ns_sem)
    await_bytes(nb.at[0 : NC - 1], nr_sem)
    for j in range(4):
        normal_out[:, 128 * j : 128 * j + 128] = (
            nb[4 * j] + nb[4 * j + 1] + nb[4 * j + 2] + nb[4 * j + 3]
        )


def shards(
    x_window, y_window, block_order, diag_inverse, panel_window, panel_trail, x_trail, y_trail
):
    vmem = pl.BlockSpec(memory_space=pltpu.VMEM)
    hbm = pl.BlockSpec(memory_space=pl.ANY)
    dma = pltpu.SemaphoreType.DMA
    white, trail, normal, right = pl.pallas_call(
        kernel,
        name="substitution",
        out_shape=(
            jax.ShapeDtypeStruct((3, 48, 128), F32),
            jax.ShapeDtypeStruct((48, 128), F32),
            jax.ShapeDtypeStruct((16, 512), F32),
            jax.ShapeDtypeStruct((16, 128), F32),
        ),
        in_specs=[pl.BlockSpec(memory_space=pltpu.SMEM), vmem, vmem, hbm, vmem, vmem],
        out_specs=(vmem, vmem, vmem, vmem),
        scratch_shapes=[
            pltpu.VMEM((3, 2, 16, 128), BF16),
            pltpu.VMEM((3, 1, 128), F32),
            pltpu.VMEM((3, 32, 16, 128), BF16),
            pltpu.VMEM((3, 32, 1, 128), F32),
            pltpu.VMEM((32, 2048), BF16),
            pltpu.VMEM((128, 128), BF16),
            pltpu.VMEM((64, 128), BF16),
            pltpu.VMEM((64, 2048), BF16),
            pltpu.VMEM((2048, 128), BF16),
            pltpu.VMEM((5, 32, 2048), BF16),
            pltpu.VMEM((5, 1, 2048), F32),
            pltpu.VMEM((3, 16, 2048), BF16),
            pltpu.VMEM((3, 128, 2048), BF16),
            pltpu.VMEM((2, 128, 2048), BF16),
            pltpu.VMEM((3, 128, 2048), BF16),
            pltpu.VMEM((3, 16, 2, 16, 128), BF16),
            pltpu.VMEM((16, 16, 128), F32),
            pltpu.VMEM((16, 16, 128), F32),
            pltpu.VMEM((16, 16, 128), F32),
            pltpu.VMEM((40, 128), F32),
            dma((1,)),
            dma,
            dma,
            dma,
            dma,
            dma((4,)),
            dma((4,)),
            dma((3,)),
            dma((3,)),
            dma((2,)),
            dma((2,)),
            dma,
            dma((16,)),
            dma((5,)),
            dma((5,)),
            dma,
            dma,
            dma((5,)),
            dma((5,)),
            dma((3,)),
            dma((3,)),
            dma((3,)),
            dma((3,)),
            dma((3,)),
            dma((3,)),
            dma((3,)),
            dma((3,)),
            dma,
            dma,
            dma,
            dma,
        ],
        compiler_params=pltpu.CompilerParams(
            collective_id=0, has_side_effects=True, vmem_limit_bytes=58 * 1024 * 1024
        ),
    )(
        block_order,
        x_window.transpose(0, 2, 1),
        y_window,
        diag_inverse,
        panel_window,
        panel_trail.transpose(1, 0, 2),
    )
    whitened = white[:, 0:32, 0:64].transpose(0, 2, 1).astype(BF16)
    white_resp = white[:, 32, 0:64].astype(BF16)
    trail_rhs = x_trail.astype(F32) - trail[0:32].T
    trail_resp = y_trail - trail[32]
    return whitened, white_resp, trail_rhs, trail_resp, normal, right[:, 0]


def solution(mesh):
    in_specs = (
        P(None, "row", "col"),
        P(None, "row"),
        P(),
        P(None, "row", None),
        P(None, "row", "col"),
        P("row", None, "col"),
        P("row", "col"),
        P("row"),
    )
    out_specs = (
        P(None, "row", "col"),
        P(None, "row"),
        P("row", "col"),
        P("row"),
        P("row", None),
        P("row"),
    )
    return jax.shard_map(shards, mesh=mesh, in_specs=in_specs, out_specs=out_specs, check_vma=False)
```

```python
import jax
import jax.numpy as jnp
from jax import lax
from jax.experimental import pallas as pl
from jax.experimental.pallas import tpu as pltpu
from jax.sharding import PartitionSpec as P

MESH = pl.DeviceIdType.MESH
F32 = jnp.float32
BF16 = jnp.bfloat16
NZ = 16
NC = 16
W0, R1, R2, W1, W2 = range(5)
WHITE = (W0, W1, W2)


def dot_t(a, b):
    return lax.dot_general(a, b, (((1,), (1,)), ((), ())), preferred_element_type=F32)


def dot_n(a, b):
    return lax.dot_general(a, b, (((1,), (0,)), ((), ())), preferred_element_type=F32)


def rounded(value):
    return value.astype(BF16).astype(F32)


def await_bytes(ref, sem):
    pltpu.make_async_copy(ref, ref, sem).wait()


def repeat(count, body):
    def step(k, carry):
        body(k)
        return carry

    lax.fori_loop(0, count, step, 0)


def kernel(
    order,
    x_ref,
    y_ref,
    d_ref,
    l_ref,
    t_ref,
    white_out,
    trail_out,
    normal_out,
    right_out,
    xsrc,
    ysrc,
    xbuf,
    ybuf,
    xr,
    ltsrc,
    ltex,
    lg,
    mv,
    gx,
    gy,
    hx,
    dv,
    lv,
    tv,
    wp,
    gp,
    gq,
    nb,
    tmp,
    own_sem,
    xs_sem,
    xr_sem,
    ys_sem,
    yr_sem,
    es_sem,
    er_sem,
    ds_sem,
    dr_sem,
    ls_sem,
    lr_sem,
    gs_sem,
    gr_sem,
    zs_sem,
    zr_sem,
    ms_sem,
    mr_sem,
    qs_sem,
    qr_sem,
    hs_sem,
    hr_sem,
    ts_sem,
    tr_sem,
    vs_sem,
    vr_sem,
    as_sem,
    ar_sem,
    rs_sem,
    rr_sem,
    ns_sem,
    nr_sem,
):
    row = lax.axis_index("row")
    c = lax.axis_index("col")
    z = row // 2
    x = row % 2
    spot = x * NC + c
    beside = {"row": 2 * z + 1 - x, "col": c}

    def far(k):
        half = (k + 1) // 2
        return lax.rem(z + NZ // 2 + jnp.where(k % 2 == 1, half, NZ - half), NZ)

    def along(k):
        return {"row": 2 * far(k) + x, "col": c}

    def across(k):
        return {"row": 2 * far(k) + 1 - x, "col": c}

    def turn(k):
        return {"row": row, "col": lax.rem(c + 1 + lax.rem(k + 8, NC - 1), NC)}

    def alike(k):
        return lax.rem(c + 2 + 2 * k, NC)

    sibling = {"row": row, "col": c + 1 - 2 * (c % 2)}

    def over(k):
        return {"row": 2 * z + 1 - x, "col": lax.rem(c + k, NC)}

    def plane(k):
        other = lax.rem(spot + 1 + lax.rem(k + 9, 2 * NC - 1), 2 * NC)
        return {"row": 2 * z + other // NC, "col": other % NC}

    def push(src, dst, send_sem, recv_sem, peer):
        pltpu.make_async_remote_copy(src, dst, send_sem, recv_sem, peer, MESH).start()

    at_c = pl.ds(pl.multiple_of(128 * c, 128), 128)
    at_z = pl.ds(pl.multiple_of(128 * z, 128), 128)
    own_half = pl.ds(pl.multiple_of(64 * x, 64), 64)
    other_half = pl.ds(pl.multiple_of(64 - 64 * x, 64), 64)

    barrier = pltpu.get_barrier_semaphore()

    def greet(peer):
        pl.semaphore_signal(barrier, inc=1, device_id=peer, device_id_type=MESH)

    repeat(NZ - 1, lambda k: greet(along(k)))
    repeat(NZ - 1, lambda k: greet(across(k)))
    repeat(2 * NC - 1, lambda k: greet(plane(k)))

    pltpu.make_async_copy(d_ref, dv.at[:, own_half, :], own_sem.at[0]).start()
    for t in range(2):
        pltpu.make_async_copy(l_ref.at[t], lv.at[t, own_half, at_c], lr_sem.at[t]).start()

    lane = lax.broadcasted_iota(jnp.int32, (16, 128), 1)
    first = x == 0
    mine = jnp.where(first, lane, 127 - lane) < 64
    mine1 = mine[0:1]

    tmp[...] = jnp.zeros_like(tmp)
    for s in range(3):
        tmp[0:32, 0:64] = x_ref[order[s]].astype(F32)
        tmp[32:33, 0:64] = y_ref[pl.ds(order[s], 1), :]
        both = tmp[...]
        both = jnp.where(first, both, pltpu.roll(both, 64, 1))
        xsrc[s, 0] = jnp.where(first, both[0:16], both[16:32]).astype(BF16)
        xsrc[s, 1] = jnp.where(first, both[16:32], both[0:16]).astype(BF16)
        ysrc[s] = both[32:33]
    eye = (
        lax.broadcasted_iota(jnp.int32, (128, 128), 0)
        == lax.broadcasted_iota(jnp.int32, (128, 128), 1)
    ).astype(F32).astype(BF16)
    lane_l = lax.broadcasted_iota(jnp.int32, (128, 128), 1)
    mine_l = jnp.where(first, lane_l, 127 - lane_l) < 64
    block = l_ref[2]
    turned = dot_t(eye, jnp.concatenate([block, block], axis=0))
    ltsrc[...] = jnp.where(mine_l, turned, 0.0).astype(BF16)

    def clear(k):
        @pl.when(k > z)
        def _():
            lg[:, pl.ds(pl.multiple_of(128 * k, 128), 128)] = jnp.zeros((64, 128), BF16)

    repeat(NZ, clear)

    xbuf[2, row] = xsrc[0, 0]
    ybuf[2, row] = ysrc[0]

    pl.semaphore_wait(barrier, 2 * (NZ - 1) + 2 * NC - 1)

    def push_x0(k):
        push(xsrc.at[0, 0], xbuf.at[2, row], xs_sem, xr_sem, along(k))
        push(xsrc.at[0, 1], xbuf.at[2, row], xs_sem, xr_sem, across(k))
        push(ysrc.at[0], ybuf.at[2, row], ys_sem, yr_sem, along(k))
        push(ysrc.at[0], ybuf.at[2, row], ys_sem, yr_sem, across(k))

    repeat(NZ - 1, push_x0)
    push(xsrc.at[0, 1], xbuf.at[2, row], xs_sem, xr_sem, beside)
    push(ysrc.at[0], ybuf.at[2, row], ys_sem, yr_sem, beside)
    push(ltsrc.at[other_half], ltex, es_sem.at[0], er_sem.at[0], beside)
    push(xsrc.at[1:3, 1], xbuf.at[0:2, 0], es_sem.at[2], er_sem.at[2], beside)
    push(ysrc.at[1:3], ybuf.at[0:2, 0], es_sem.at[3], er_sem.at[3], beside)

    def push_d(s):
        def one(k):
            push(
                d_ref.at[s, :, at_c], dv.at[s, own_half, at_c], ds_sem.at[s], dr_sem.at[s], over(k)
            )

        repeat(NC, one)

    def push_lg():
        await_bytes(ltex, er_sem.at[0])
        lg[:, at_z] = ltsrc[own_half, :] + ltex[...]

        def one(k):
            @pl.when(far(k) > z)
            def _():
                push(lg.at[:, at_z], lg.at[:, at_z], gs_sem, gr_sem.at[z], along(k))

        repeat(NZ - 1, one)

    def push_l(t):
        repeat(
            2 * NC - 1,
            lambda k: push(
                l_ref.at[t], lv.at[t, own_half, at_c], ls_sem.at[t], lr_sem.at[t], plane(k)
            ),
        )

    def form_m():
        def one(k):
            @pl.when(k < z)
            def _():
                await_bytes(lg.at[:, pl.ds(pl.multiple_of(128 * k, 128), 128)], gr_sem.at[k])

        repeat(NZ - 1, one)
        await_bytes(dv.at[2, 0:64], dr_sem.at[2])
        at = pl.ds(pl.multiple_of(128 * c + 64 * x, 64), 64)
        mv[at, :] = dot_t(lg[...], dv[2]).astype(BF16)
        repeat(2 * NC - 1, lambda k: push(mv.at[at], mv.at[at], ms_sem, mr_sem, plane(k)))

    def push_a(s):
        p = WHITE[s]
        pltpu.make_async_copy(gx.at[p, 0:16, at_z], wp.at[s, c, x], ar_sem.at[s]).start()
        repeat(
            2 * NC - 1,
            lambda k: push(
                gx.at[p, 0:16, at_z], wp.at[s, c, x], as_sem.at[s], ar_sem.at[s], plane(k)
            ),
        )

    def send(p, value):
        gx[p, 0:16, at_z] = value[0:16].astype(BF16)
        gy[p, :, at_z] = value[16:17]

        if p == W2:
            push_a(2)

        def one(k):
            push(gx.at[p, 0:16, at_z], gx.at[p, 0:16, at_z], zs_sem.at[p], zr_sem.at[p], along(k))
            push(gy.at[p, :, at_z], gy.at[p, :, at_z], qs_sem.at[p], qr_sem.at[p], along(k))
            if p == W2:
                push(gx.at[p, 0:16, at_z], hx.at[2, :, at_z], hs_sem.at[2], hr_sem.at[2], across(k))

        repeat(NZ - 1, one)
        if p == W2:
            push(gx.at[p, 0:16, at_z], hx.at[2, :, at_z], hs_sem.at[2], hr_sem.at[2], beside)

    def receive(p):
        await_bytes(gx.at[p, 0:16, 0 : 128 * (NZ - 1)], zr_sem.at[p])
        await_bytes(gy.at[p, :, 0 : 128 * (NZ - 1)], qr_sem.at[p])
        gx[p, 16:32, :] = jnp.broadcast_to(gy[p], (16, 128 * NZ)).astype(BF16)

    def push_t(s):
        def one(k):
            peer = {"row": row, "col": alike(k)}
            push(t_ref.at[s], tv.at[s, :, at_c], ts_sem.at[s], tr_sem.at[s], peer)

        repeat(NC // 2 - 1, one)
        push(t_ref.at[s], tv.at[s, :, at_c], vs_sem.at[s], vr_sem.at[s], sibling)
        tv[s, :, at_c] = t_ref[s]

    def relay_t(s):
        await_bytes(tv.at[s, :, 0 : 128 * (NC // 2 - 1)], tr_sem.at[s])

        def one(k):
            at = pl.ds(pl.multiple_of(128 * alike(k), 128), 128)
            push(tv.at[s, :, at], tv.at[s, :, at], vs_sem.at[s], vr_sem.at[s], sibling)

        repeat(NC // 2 - 1, one)

    def push_h(s):
        push(gx.at[WHITE[s], 0:16], hx.at[s], hs_sem.at[s], hr_sem.at[s], beside)

    def receive_h(s):
        await_bytes(hx.at[s], hr_sem.at[s])

    def put_white(s):
        own = gx[WHITE[s], 0:16, at_z].astype(F32)
        other = hx[s, :, at_z].astype(F32)
        resp = gx[WHITE[s], 16:32, at_z].astype(F32)
        value = jnp.concatenate(
            [jnp.where(first, own, other), jnp.where(first, other, own), resp], axis=0
        )
        white_out[s] = jnp.where(first, value, pltpu.roll(value, 64, 1)).astype(BF16)

    def trail_term(s):
        await_bytes(tv.at[s, :, 0 : 128 * (NC // 2)], vr_sem.at[s])
        return dot_t(jnp.concatenate([gx[WHITE[s]], hx[s]], axis=0), tv[s])

    def gram_term(s):
        await_bytes(wp.at[s], ar_sem.at[s])
        left = wp[s, :, x].reshape(256, 128)
        own = wp[s, c].reshape(32, 128).astype(F32)
        resp = jnp.broadcast_to(gy[WHITE[s], :, at_z], (32, 128))
        groups = [jnp.where(c % 4 == j, own, resp) for j in range(4)]
        return dot_t(left, jnp.concatenate(groups, axis=0).astype(BF16))

    push_d(0)
    push_l(0)
    push_lg()
    await_bytes(xbuf.at[0:2, 0], er_sem.at[2])
    await_bytes(ybuf.at[0:2, 0], er_sem.at[3])
    starts = []
    for s in range(1, 3):
        tile = xsrc[s, 0].astype(F32) + xbuf[s - 1, 0].astype(F32)
        resp = jnp.broadcast_to(ysrc[s] + ybuf[s - 1, 0], (16, 128))
        starts.append(jnp.concatenate([tile, resp], axis=0))
    await_bytes(dv.at[:, 0:64, :], own_sem.at[0])

    await_bytes(xbuf.at[2, 0 : 2 * NZ - 1], xr_sem)
    await_bytes(ybuf.at[2, 0 : 2 * NZ - 1], yr_sem)
    for k in range(NZ):
        xr[0:16, 128 * k : 128 * k + 128] = xbuf[2, 2 * k] + xbuf[2, 2 * k + 1]
        xr[16:32, 128 * k : 128 * k + 128] = jnp.broadcast_to(
            ybuf[2, 2 * k] + ybuf[2, 2 * k + 1], (16, 128)
        ).astype(BF16)
    await_bytes(dv.at[0, 0:64], dr_sem.at[0])
    send(W0, rounded(dot_t(xr[...], dv[0])))
    push_d(1)
    push_l(1)
    push_d(2)
    push_a(0)

    receive(W0)
    await_bytes(lv.at[0], lr_sem.at[0])
    send(R1, starts[0] - dot_t(gx[W0], lv[0]))
    form_m()
    await_bytes(lv.at[1], lr_sem.at[1])
    send(R2, starts[1] - dot_t(gx[W0], lv[1]))
    push_h(0)

    await_bytes(dv.at[1, 0:64], dr_sem.at[1])
    receive(R1)
    send(W1, rounded(dot_t(gx[R1], dv[1])))
    push_a(1)
    for s in range(3):
        push_t(s)
    receive(R2)
    value2 = dot_t(gx[R2], dv[2])
    receive_h(0)
    put_white(0)
    gram = gram_term(0)

    receive(W1)
    await_bytes(mv.at[0 : 64 * (2 * NC - 1)], mr_sem)
    send(W2, rounded(value2 - dot_n(gx[W1], mv[...])))
    push_h(1)
    gram = gram + gram_term(1)

    gram = (gram + gram_term(2)) * (1.0 / 6144)
    gp[...] = gram.reshape(16, 16, 128)
    repeat(NZ - 1, lambda k: push(gp.at[far(k)], gq.at[z], rs_sem, rr_sem, along(k)))
    gq[z] = gp[z]
    for s in range(3):
        relay_t(s)
    trail = trail_term(0)
    receive_h(1)
    put_white(1)
    trail = trail + trail_term(1)

    receive(W2)
    receive_h(2)
    put_white(2)
    trail = trail + trail_term(2)
    trail_out[0:16] = jnp.where(first, trail[0:16], trail[32:48])
    trail_out[16:32] = jnp.where(first, trail[32:48], trail[0:16])
    trail_out[32:48] = trail[16:32]
    await_bytes(gq.at[0 : NZ - 1], rr_sem)
    gram = gq[0]
    for k in range(1, NZ):
        gram = gram + gq[k]
    nb[c] = jnp.where(lane // 32 == c % 4, gram, 0.0)
    repeat(NC - 1, lambda k: push(nb.at[c], nb.at[c], ns_sem, nr_sem, turn(k)))
    spare = jnp.where(c % 4 == 0, 32, 0)
    right = jnp.sum(jnp.where(lane == spare, gram, 0.0), axis=1, keepdims=True)
    right_out[...] = jnp.broadcast_to(right, (16, 128))
    await_bytes(gq.at[0 : NZ - 1], rs_sem)

    await_bytes(xbuf.at[2, 0 : 2 * NZ - 1], xs_sem)
    await_bytes(ybuf.at[2, 0 : 2 * NZ - 1], ys_sem)
    await_bytes(ltex, es_sem.at[0])
    repeat(NZ - 1 - z, lambda k: await_bytes(lg.at[:, 0:128], gs_sem))
    await_bytes(mv.at[0 : 64 * (2 * NC - 1)], ms_sem)
    await_bytes(xbuf.at[0:2, 0], es_sem.at[2])
    await_bytes(ybuf.at[0:2, 0], es_sem.at[3])
    for t in range(2):
        repeat(2 * NC - 1, lambda k: await_bytes(lv.at[t, 0:64, 0:128], ls_sem.at[t]))
    for p in range(5):
        await_bytes(gx.at[p, 0:16, 0 : 128 * (NZ - 1)], zs_sem.at[p])
        await_bytes(gy.at[p, :, 0 : 128 * (NZ - 1)], qs_sem.at[p])
    for s in range(3):
        await_bytes(dv.at[s, 0:64], ds_sem.at[s])
        await_bytes(hx.at[s], hs_sem.at[s])
        await_bytes(tv.at[s, :, 0 : 128 * (NC // 2 - 1)], ts_sem.at[s])
        await_bytes(tv.at[s, :, 0 : 128 * (NC // 2)], vs_sem.at[s])

        repeat(2 * NC - 1, lambda k: await_bytes(wp.at[s, 0, 0], as_sem.at[s]))

    await_bytes(nb.at[0 : NC - 1], ns_sem)
    await_bytes(nb.at[0 : NC - 1], nr_sem)
    for j in range(4):
        normal_out[:, 128 * j : 128 * j + 128] = (
            nb[4 * j] + nb[4 * j + 1] + nb[4 * j + 2] + nb[4 * j + 3]
        )


def shards(
    x_window, y_window, block_order, diag_inverse, panel_window, panel_trail, x_trail, y_trail
):
    vmem = pl.BlockSpec(memory_space=pltpu.VMEM)
    hbm = pl.BlockSpec(memory_space=pl.ANY)
    dma = pltpu.SemaphoreType.DMA
    white, trail, normal, right = pl.pallas_call(
        kernel,
        name="substitution",
        out_shape=(
            jax.ShapeDtypeStruct((3, 48, 128), BF16),
            jax.ShapeDtypeStruct((48, 128), F32),
            jax.ShapeDtypeStruct((16, 512), F32),
            jax.ShapeDtypeStruct((16, 128), F32),
        ),
        in_specs=[pl.BlockSpec(memory_space=pltpu.SMEM), vmem, vmem, hbm, vmem, vmem],
        out_specs=(vmem, vmem, vmem, vmem),
        scratch_shapes=[
            pltpu.VMEM((3, 2, 16, 128), BF16),
            pltpu.VMEM((3, 1, 128), F32),
            pltpu.VMEM((3, 32, 16, 128), BF16),
            pltpu.VMEM((3, 32, 1, 128), F32),
            pltpu.VMEM((32, 2048), BF16),
            pltpu.VMEM((128, 128), BF16),
            pltpu.VMEM((64, 128), BF16),
            pltpu.VMEM((64, 2048), BF16),
            pltpu.VMEM((2048, 128), BF16),
            pltpu.VMEM((5, 32, 2048), BF16),
            pltpu.VMEM((5, 1, 2048), F32),
            pltpu.VMEM((3, 16, 2048), BF16),
            pltpu.VMEM((3, 128, 2048), BF16),
            pltpu.VMEM((2, 128, 2048), BF16),
            pltpu.VMEM((3, 128, 2048), BF16),
            pltpu.VMEM((3, 16, 2, 16, 128), BF16),
            pltpu.VMEM((16, 16, 128), F32),
            pltpu.VMEM((16, 16, 128), F32),
            pltpu.VMEM((16, 16, 128), F32),
            pltpu.VMEM((40, 128), F32),
            dma((1,)),
            dma,
            dma,
            dma,
            dma,
            dma((4,)),
            dma((4,)),
            dma((3,)),
            dma((3,)),
            dma((2,)),
            dma((2,)),
            dma,
            dma((16,)),
            dma((5,)),
            dma((5,)),
            dma,
            dma,
            dma((5,)),
            dma((5,)),
            dma((3,)),
            dma((3,)),
            dma((3,)),
            dma((3,)),
            dma((3,)),
            dma((3,)),
            dma((3,)),
            dma((3,)),
            dma,
            dma,
            dma,
            dma,
        ],
        compiler_params=pltpu.CompilerParams(
            collective_id=0, has_side_effects=True, vmem_limit_bytes=58 * 1024 * 1024
        ),
    )(
        block_order,
        x_window.transpose(0, 2, 1),
        y_window,
        diag_inverse,
        panel_window,
        panel_trail.transpose(1, 0, 2),
    )
    whitened = white[:, 0:32, 0:64].transpose(0, 2, 1)
    white_resp = white[:, 32, 0:64]
    trail_rhs = x_trail.astype(F32) - trail[0:32].T
    trail_resp = y_trail - trail[32]
    return whitened, white_resp, trail_rhs, trail_resp, normal, right[:, 0]


def solution(mesh):
    in_specs = (
        P(None, "row", "col"),
        P(None, "row"),
        P(),
        P(None, "row", None),
        P(None, "row", "col"),
        P("row", None, "col"),
        P("row", "col"),
        P("row"),
    )
    out_specs = (
        P(None, "row", "col"),
        P(None, "row"),
        P("row", "col"),
        P("row"),
        P("row", None),
        P("row"),
    )
    return jax.shard_map(shards, mesh=mesh, in_specs=in_specs, out_specs=out_specs, check_vma=False)
```
